512 devices in a mesh: ctx: 64 (over z, x), head: 8 (over y, core).
Axes of the slice: x: 4, y: 4, z: 16, core: 2. Of those that a mesh axis runs over, the one named last changes fastest.
Arguments:
- queries: bfloat16 [8192, 8192], P('ctx', 'head'), may hold values from -6 to 6
- keys: bfloat16 [8192, 8192], P('ctx', 'head'), may hold values from -6 to 6
- values: bfloat16 [8192, 8192], P('ctx', 'head'), may hold values from -6 to 6
- log_decay: float32 [8192, 64], P('ctx', 'head'), may hold values from -1 to 0, as said below
- gain: float32 [8192], P('head'), may hold values from 0.1 to 1.9
- grad_out: bfloat16 [8192, 8192], P('ctx', 'head'), may hold values from -6 to 6
Outputs:
- normed: bfloat16 [8192, 8192], P('ctx', 'head')
- grad_queries: bfloat16 [8192, 8192], P('ctx', 'head')
- grad_keys: bfloat16 [8192, 8192], P('ctx', 'head')
- grad_values: bfloat16 [8192, 8192], P('ctx', 'head')
The draws below stay inside these ranges and needn't reach their ends.
Inputs may be any that keep to these rules, and one draw needn't show every extreme that they name: `log_decay`: entries are negative.
All inputs are finite; a program needn't handle non-finite values.
Results may differ from the reference program's by a relative error of at most 0.0095.
Values sent between devices are 32-bit elements; how exact they have to be, the bound alone decides.
A program may use at most 128 MiB of HBM per device.

```python
import math
import jax
import jax.numpy as jnp
from jax import lax

HEADS = 64
HEAD_DIM = 128
TOK_DEV = 128
TOKEN_LENGTH = 8192
WIDTH = 8192
N_CTX = 64


def draw_log_decay(key, part):
    sequence_batch = jax.random.split(jax.random.fold_in(key, 7), 7)
    slow_rate = jax.random.uniform(sequence_batch[0], (HEADS,), jnp.float32, 0.05, 0.8) / TOKEN_LENGTH
    fast_rate = jnp.exp(jax.random.uniform(sequence_batch[1], (HEADS,), jnp.float32, math.log(1.0 / 50.0), math.log(1.0 / 25.0)))
    fast_share = 0.5
    is_fast = jax.random.uniform(sequence_batch[2], (HEADS,), jnp.float32) < fast_share
    baseline_decay_rate = jnp.where(is_fast, fast_rate, slow_rate)
    coarse_estimate = jnp.exp(jax.random.uniform(sequence_batch[3], (TOKEN_LENGTH, HEADS), jnp.float32, -0.7, 0.7))
    region_count = TOKEN_LENGTH // TOK_DEV
    region_factor = jnp.exp(jax.random.uniform(sequence_batch[4], (region_count, HEADS), jnp.float32, -0.7, 0.7))
    segment_rows = jnp.repeat(region_factor, TOK_DEV, axis=0)
    spike_location = jax.random.randint(sequence_batch[5], (2,), 0, TOKEN_LENGTH)
    spike_retention = jax.random.uniform(sequence_batch[6], (2,), jnp.float32, 0.5, 0.8)
    token_position = jnp.arange(TOKEN_LENGTH)
    spike_log_decay = jnp.sum(jnp.where(token_position[:, None] == spike_location[None, :], jnp.log(spike_retention)[None, :], 0.0), axis=1)
    return -baseline_decay_rate[None, :] * coarse_estimate * segment_rows + spike_log_decay[:, None]


def steps_of(rng, shape, cuts, least, largest):
    level, own = 1.0, jax.random.fold_in(rng, 6)
    for axis_at, shards_of in cuts:
        draws = jnp.exp(jax.random.uniform(jax.random.fold_in(own, axis_at), (shards_of,), jnp.float32, least / len(cuts), largest / len(cuts)))
        level = level * jnp.repeat(draws, shape[axis_at] // shards_of).reshape([-1 if axis == axis_at else 1 for axis in range(len(shape))])
    return level


def gaussian(own_key, shape, deviation, bound, pieces=(), held_as=jnp.bfloat16):
    loudness = steps_of(own_key, shape, pieces, -0.22, 0.18) if pieces else 1.0
    drawn = jax.random.normal(own_key, shape, jnp.float32) * deviation * loudness
    return jnp.minimum(jnp.maximum(drawn, -bound), bound).astype(held_as)


def setup_inputs(seed: int = 0) -> dict:
    key_of = jax.random.split(jax.random.key(seed), 7)
    queries = gaussian(key_of[0], (TOKEN_LENGTH, WIDTH), 1.0, 6.0, ((0, 64), (1, 8)))
    keys = gaussian(key_of[1], (TOKEN_LENGTH, WIDTH), 1.0, 6.0, ((0, 64), (1, 8)))
    values = gaussian(key_of[2], (TOKEN_LENGTH, WIDTH), 1.0, 6.0, ((0, 64), (1, 8)))
    log_decay = draw_log_decay(jax.random.fold_in(key_of[6], 71), 0)
    gain = jnp.clip(1.0 + 0.18 * jax.random.normal(key_of[4], (WIDTH,), jnp.float32), 0.1, 1.9)
    grad_out = gaussian(key_of[5], (TOKEN_LENGTH, WIDTH), 1.0, 6.0, ((0, 64), (1, 8)))
    return {"queries": queries, "keys": keys, "values": values, "log_decay": log_decay, "gain": gain, "grad_out": grad_out}


epsilon = 1e-06

def block_decays(log_block):
    cumulative = jnp.cumsum(log_block, axis=0)
    last_log = cumulative[-1]
    log_rows = cumulative.T
    spread = log_rows[:, :, None] - log_rows[:, None, :]
    count = log_block.shape[0]
    token_position = lax.broadcasted_iota(jnp.int32, (count, count), 0)
    source = lax.broadcasted_iota(jnp.int32, (count, count), 1)
    decay_matrix = jnp.where((token_position >= source)[None], jnp.exp(jnp.minimum(spread, 0.0)), 0.0)
    return (cumulative, last_log, decay_matrix)

def block_terms(query_block, key_block, value_block, log_block):
    cumulative, last_log, decay_matrix = block_decays(log_block)
    query_float = query_block.astype(jnp.float32)
    key_float = key_block.astype(jnp.float32)
    value_float = value_block.astype(jnp.float32)
    scores = jnp.einsum('thd,shd->hts', query_float, key_float)
    weights = lax.optimization_barrier((scores * decay_matrix).astype(jnp.bfloat16))
    intra_out = jnp.einsum('hts,shd->thd', weights.astype(jnp.float32), value_float)
    key_decay = jnp.exp(last_log[None, :] - cumulative)
    key_scaled = lax.optimization_barrier((key_decay[:, :, None] * key_float).astype(jnp.bfloat16))
    local_state = jnp.einsum('thd,the->hde', key_scaled.astype(jnp.float32), value_float, precision=lax.Precision.HIGHEST)
    query_decay = jnp.exp(cumulative)
    query_scaled = query_decay[:, :, None] * query_float
    return (weights, intra_out, key_decay, key_scaled, local_state, query_decay, query_scaled, jnp.exp(last_log), decay_matrix, query_float, key_float, value_float)

def reference(queries, keys, values, log_decay, gain, grad_out):
    shape_four = (N_CTX, TOK_DEV, HEADS, HEAD_DIM)
    query_blocks = queries.reshape(shape_four)
    key_blocks = keys.reshape(shape_four)
    value_blocks = values.reshape(shape_four)
    log_blocks = log_decay.reshape(N_CTX, TOK_DEV, HEADS)

    def forward_step(state, inputs):
        terms = block_terms(*inputs)
        inter_out = jnp.einsum('thd,hde->the', terms[6], state, precision=lax.Precision.HIGHEST)
        new_state = terms[7][:, None, None] * state + terms[4]
        return (new_state, (terms[1] + inter_out, state))
    start = jnp.zeros((HEADS, HEAD_DIM, HEAD_DIM), jnp.float32)
    _, (attended, entering) = lax.scan(forward_step, start, (query_blocks, key_blocks, value_blocks, log_blocks))
    attended = attended.reshape(TOKEN_LENGTH, HEADS * HEAD_DIM)
    total_width = HEADS * HEAD_DIM
    squares = lax.optimization_barrier(jnp.sum(attended * attended, axis=1))
    inverse = lax.rsqrt(squares / total_width + epsilon)
    normed = (attended * inverse[:, None] * gain[None, :]).astype(jnp.bfloat16)
    scaled_grad = grad_out.astype(jnp.float32) * gain[None, :]
    products = lax.optimization_barrier(jnp.sum(scaled_grad * attended, axis=1))
    grad_attended = (inverse[:, None] * scaled_grad - attended * (inverse ** 3 * products / total_width)[:, None]).astype(jnp.bfloat16)
    grad_blocks = grad_attended.reshape(shape_four)

    def backward_step(later, inputs):
        query_block, key_block, value_block, log_block, grad_block, entering_block = inputs
        weights, intra_out, key_decay, key_scaled, local_state, query_decay, query_scaled, block_decay, decay_matrix, query_float, key_float, value_float = block_terms(query_block, key_block, value_block, log_block)
        grad_float = grad_block.astype(jnp.float32)
        grad_state = jnp.einsum('thd,the->hde', query_scaled, grad_float, precision=lax.Precision.HIGHEST)
        grad_weights = jnp.einsum('the,she->hts', grad_float, value_float)
        grad_scores = lax.optimization_barrier((grad_weights * decay_matrix).astype(jnp.bfloat16)).astype(jnp.float32)
        grad_query = jnp.einsum('hts,shd->thd', grad_scores, key_float) + query_decay[:, :, None] * jnp.einsum('the,hde->thd', grad_float, entering_block, precision=lax.Precision.HIGHEST)
        grad_key = jnp.einsum('hts,thd->shd', grad_scores, query_float) + key_decay[:, :, None] * jnp.einsum('she,hde->shd', value_float, later, precision=lax.Precision.HIGHEST)
        grad_value = jnp.einsum('hts,thd->shd', weights.astype(jnp.float32), grad_float) + jnp.einsum('shd,hde->she', key_scaled.astype(jnp.float32), later, precision=lax.Precision.HIGHEST)
        new_later = grad_state + block_decay[:, None, None] * later
        return (new_later, (grad_query.astype(jnp.bfloat16), grad_key.astype(jnp.bfloat16), grad_value.astype(jnp.bfloat16)))
    _, (grad_q, grad_k, grad_v) = lax.scan(backward_step, start, (query_blocks, key_blocks, value_blocks, log_blocks, grad_blocks, entering), reverse=True)
    flat = (TOKEN_LENGTH, HEADS * HEAD_DIM)
    return (normed, grad_q.reshape(flat), grad_k.reshape(flat), grad_v.reshape(flat))
```

```python
import functools

import jax
import jax.numpy as jnp
from jax import lax
from jax.experimental import pallas as pl
from jax.experimental.pallas import tpu as pltpu
from jax.sharding import Mesh
from jax.sharding import PartitionSpec as P

HEADS = 64
HEAD_DIM = 128
GROUP = 8
GROUPS = 8
PARTS = 2
LOCAL_HEADS = 8
PART_HEADS = LOCAL_HEADS // PARTS
SLICE = HEAD_DIM // GROUP
ROWS = PART_HEADS * SLICE
SUB = ROWS // GROUPS
FAR_FIRST = (4, 3, 5, 2, 6, 1, 7)
AXES = ("zh", "zl", "x", "head")
MESH = pl.DeviceIdType.MESH

epsilon = 1e-06


def dot(a, b, ca, cb, precision=None):
    return lax.dot_general(
        a, b, (((ca,), (cb,)), ((), ())), preferred_element_type=jnp.float32, precision=precision
    )


def kernel(
    q_hbm, k_hbm, v_hbm, log_ref, gain_ref, g_hbm,
    normed_out, gq_out, gk_out, gv_out,
    q_ref, k_ref, v_ref, g_ref, n_ref, gq_ref, gk_ref, gv_ref,
    decay_ref, kd_ref, qd_ref, ks_ref, qst_ref, w_ref, att_ref, sg_ref, ga_ref, s_ref, gki_ref, gvi_ref,
    a_send, a_recv, z_send, z_recv, y_send, y_recv, b_send, b_recv,
    a2_send, a2_recv, z2_send, z2_recv, y2_send, y2_recv, b2_send, b2_recv,
    h_send, h_recv, in_sem, out_sem, send_sem, recv_sem,
):
    zh, zl, x, head = (lax.axis_index(a) for a in AXES)
    me = zl * 4 + x

    def group_device(j):
        return (zh, lax.div(j, 4), lax.rem(j, 4), head)

    def groups_device(j):
        return (j, zl, x, head)

    def head_device(j):
        return (zh, zl, x, j)

    def copies(src, dst, mine, device, slot, arriving):
        for k in FAR_FIRST:
            j = lax.rem(mine + (8 - k if arriving else k), 8)
            yield pltpu.make_async_remote_copy(
                src_ref=src(j),
                dst_ref=dst(j if arriving else mine),
                send_sem=send_sem.at[slot, k - 1],
                recv_sem=recv_sem.at[slot, k - 1],
                device_id=device(j),
                device_id_type=MESH,
            )

    def exchange(src, dst, mine, device, slot):
        for c in copies(src, dst, mine, device, slot, False):
            c.start()

    def arrived(src, dst, mine, device, slot):
        for c in copies(src, dst, mine, device, slot, True):
            c.wait_recv()

    def sent(src, dst, mine, device, slot):
        for c in copies(src, dst, mine, device, slot, False):
            c.wait_send()

    barrier = pltpu.get_barrier_semaphore()
    for mine, device in ((zh, groups_device), (me, group_device), (head, head_device)):
        for k in FAR_FIRST:
            pl.semaphore_signal(
                barrier, inc=1, device_id=device(lax.rem(mine + k, 8)), device_id_type=MESH
            )
    loads = [
        pltpu.make_async_copy(a, b, in_sem.at[i])
        for i, (a, b) in enumerate(((k_hbm, k_ref), (v_hbm, v_ref), (q_hbm, q_ref), (g_hbm, g_ref)))
    ]
    for c in loads:
        c.start()

    def cols(h):
        return slice(h * HEAD_DIM, (h + 1) * HEAD_DIM)

    n = HEAD_DIM
    row = lax.broadcasted_iota(jnp.int32, (n, n), 0)
    col = lax.broadcasted_iota(jnp.int32, (n, n), 1)
    log_rows = jnp.concatenate(
        [log_ref[...], jnp.zeros((n, n - LOCAL_HEADS), jnp.float32)], axis=1
    ).T[:LOCAL_HEADS]
    upto = jnp.where(row <= col, 1.0, 0.0).astype(jnp.float32)
    cum = dot(log_rows, upto, 1, 0, lax.Precision.HIGHEST)
    last = jnp.broadcast_to(cum[:, n - 1 :], (LOCAL_HEADS, n))
    block_decay = jnp.exp(last)

    def across(r):
        return jnp.broadcast_to(r, (n, n))

    def plan(s, r, mine, device, slot):
        return (s, r, mine, device, slot)

    def at(ref, c):
        return lambda j: ref.at[c, j]

    plans = {}
    slot = 0
    for name, (s, r, mine, device) in {
        "a": (a_send, a_recv, me, group_device),
        "z": (z_send, z_recv, zh, groups_device),
        "y": (y_send, y_recv, zh, groups_device),
        "b": (b_send, b_recv, me, group_device),
        "a2": (a2_send, a2_recv, me, group_device),
        "z2": (z2_send, z2_recv, zh, groups_device),
        "y2": (y2_send, y2_recv, zh, groups_device),
        "b2": (b2_send, b2_recv, me, group_device),
    }.items():
        for c in range(PARTS):
            plans[name, c] = (at(s, c), at(r, c), mine, device, slot)
            slot += 1
    plans["h"] = (lambda j: h_send, lambda j: h_recv.at[j], head, head_device, slot)

    def go(name, c, s, r, mine):
        r[c, mine] = s[c, mine]
        exchange(*plans[name, c])

    loads[0].wait()
    loads[1].wait()
    for c in range(PARTS):
        for i in range(PART_HEADS):
            h = c * PART_HEADS + i
            cum_col = across(cum[h : h + 1]).T
            key_decay = jnp.exp(last[h : h + 1] - cum_col)
            kd_ref[h] = key_decay
            qd_ref[h] = jnp.exp(cum_col)
            ks = (key_decay * k_ref[:, cols(h)].astype(jnp.float32)).astype(jnp.bfloat16)
            ks_ref[h] = ks
            decay_ref[h] = jnp.where(
                row >= col, jnp.exp(jnp.minimum(cum_col - across(cum[h : h + 1]), 0.0)), 0.0
            )
            state = dot(ks, v_ref[:, cols(h)], 0, 0)
            a_send[c, :, i * SLICE : (i + 1) * SLICE, :] = state.reshape(GROUP, SLICE, n)
        a_send[c, :, ROWS:, :] = jnp.broadcast_to(block_decay[None], (GROUP, LOCAL_HEADS, n))
        if c == 0:
            pl.semaphore_wait(barrier, 21)
        go("a", c, a_send, a_recv, me)

    loads[2].wait()
    loads[3].wait()

    def forward_local(h):
        q = q_ref[:, cols(h)]
        w = (dot(q, k_ref[:, cols(h)], 1, 1) * decay_ref[h]).astype(jnp.bfloat16)
        w_ref[h] = w
        att_ref[h] = dot(w, v_ref[:, cols(h)], 1, 0)

    def forward_more(h):
        qst_ref[h] = (qd_ref[h] * q_ref[:, cols(h)].astype(jnp.float32)).T.astype(jnp.bfloat16)
        sg_ref[h] = g_ref[:, cols(h)].astype(jnp.float32) * gain_ref[:, cols(h)]

    for h in range(LOCAL_HEADS):
        forward_local(h)

    def decay_of(c, j, i):
        h = c * PART_HEADS + i
        return a_recv[c, j, ROWS + h : ROWS + h + 1, :]

    def part(i):
        return slice(i * SLICE, (i + 1) * SLICE)

    forward = range(8)
    backward = range(7, -1, -1)

    for c in range(PARTS):
        arrived(*plans["a", c])
        folded, decays = [], []
        for i in range(PART_HEADS):
            total = a_recv[c, 0, part(i), :]
            decay = decay_of(c, 0, i)
            for j in range(1, GROUP):
                d = decay_of(c, j, i)
                total = d * total + a_recv[c, j, part(i), :]
                decay = d * decay
            folded.append(total)
            decays.append(jnp.broadcast_to(decay, (SLICE * 8 // SUB, n)))
        z_send[c, :, :SUB, :] = jnp.concatenate(folded, axis=0).reshape(GROUPS, SUB, n)
        z_send[c, :, SUB:, :] = jnp.concatenate(decays, axis=0).reshape(GROUPS, 8, n)
        go("z", c, z_send, z_recv, zh)

    for h in range(LOCAL_HEADS):
        forward_more(h)

    for c in range(PARTS):
        arrived(*plans["z", c])
        state = jnp.zeros((SUB, n), jnp.float32)
        for g in forward:
            y_send[c, g] = state
            state = z_recv[c, g, SUB : SUB + 1, :] * state + z_recv[c, g, :SUB, :]
        go("y", c, y_send, y_recv, zh)

    for c in range(PARTS):
        arrived(*plans["y", c])
        entering = y_recv[c].reshape(ROWS, n)
        for i in range(PART_HEADS):
            state = entering[part(i)]
            for j in forward:
                b_send[c, j, part(i), :] = state
                state = decay_of(c, j, i) * state + a_recv[c, j, part(i), :]
        go("b", c, b_send, b_recv, me)

    squares = jnp.zeros((n, n), jnp.float32)
    products = jnp.zeros((n, n), jnp.float32)
    for c in range(PARTS):
        arrived(*plans["b", c])
        for i in range(PART_HEADS):
            h = c * PART_HEADS + i
            state = b_recv[c, :, part(i), :].reshape(n, n).astype(jnp.bfloat16)
            s_ref[h] = state
            att = att_ref[h] + qd_ref[h] * dot(q_ref[:, cols(h)], state, 1, 0)
            att_ref[h] = att
            squares += att * att
            products += sg_ref[h] * att

    ones = jnp.ones((8, n), jnp.float32)
    sums = jnp.where(
        lax.broadcasted_iota(jnp.int32, (8, n), 0) == 0,
        dot(ones, squares, 1, 1, lax.Precision.HIGHEST),
        dot(ones, products, 1, 1, lax.Precision.HIGHEST),
    )
    h_send[...] = sums
    h_recv[head] = sums
    exchange(*plans["h"])
    arrived(*plans["h"])
    sums = h_recv[0]
    for j in range(1, 8):
        sums += h_recv[j]
    width = HEADS * HEAD_DIM
    inverse_row = lax.rsqrt(sums[0:1] / width + epsilon)
    factor_row = inverse_row * inverse_row * inverse_row * sums[1:2] / width
    inverse = across(inverse_row).T
    factor = across(factor_row).T

    for c in range(PARTS):
        for i in range(PART_HEADS):
            h = c * PART_HEADS + i
            ga = (inverse * sg_ref[h] - att_ref[h] * factor).astype(jnp.bfloat16)
            ga_ref[h] = ga
            a2_send[c, :, part(i), :] = dot(qst_ref[h], ga, 1, 0).reshape(GROUP, SLICE, n)
        go("a2", c, a2_send, a2_recv, me)

    def backward_local(h):
        ga = ga_ref[h]
        gs = (dot(ga, v_ref[:, cols(h)], 1, 1) * decay_ref[h]).astype(jnp.bfloat16)
        gq_ref[:, cols(h)] = (
            dot(gs, k_ref[:, cols(h)], 1, 0) + qd_ref[h] * dot(ga, s_ref[h], 1, 1)
        ).astype(jnp.bfloat16)
        gki_ref[h] = dot(gs, q_ref[:, cols(h)], 0, 0)
        gvi_ref[h] = dot(w_ref[h], ga, 0, 0)
        n_ref[:, cols(h)] = (att_ref[h] * inverse * gain_ref[:, cols(h)]).astype(jnp.bfloat16)

    for h in range(PART_HEADS):
        backward_local(h)

    for c in range(PARTS):
        arrived(*plans["a2", c])
        folded = []
        for i in range(PART_HEADS):
            total = a2_recv[c, GROUP - 1, part(i), :]
            for j in range(GROUP - 2, -1, -1):
                total = decay_of(c, j, i) * total + a2_recv[c, j, part(i), :]
            folded.append(total)
        z2_send[c] = jnp.concatenate(folded, axis=0).reshape(GROUPS, SUB, n)
        go("z2", c, z2_send, z2_recv, zh)

    for h in range(PART_HEADS, LOCAL_HEADS):
        backward_local(h)
    stores = [
        pltpu.make_async_copy(a, b, out_sem.at[i])
        for i, (a, b) in enumerate(
            ((n_ref, normed_out), (gq_ref, gq_out), (gk_ref, gk_out), (gv_ref, gv_out))
        )
    ]
    stores[0].start()
    stores[1].start()

    for c in range(PARTS):
        arrived(*plans["z2", c])
        state = jnp.zeros((SUB, n), jnp.float32)
        for g in backward:
            y2_send[c, g] = state
            state = z_recv[c, g, SUB : SUB + 1, :] * state + z2_recv[c, g]
        go("y2", c, y2_send, y2_recv, zh)

    for c in range(PARTS):
        arrived(*plans["y2", c])
        later = y2_recv[c].reshape(ROWS, n)
        for i in range(PART_HEADS):
            state = later[part(i)]
            for j in backward:
                b2_send[c, j, part(i), :] = state
                state = decay_of(c, j, i) * state + a2_recv[c, j, part(i), :]
        go("b2", c, b2_send, b2_recv, me)

    for key, p in plans.items():
        if key[0] != "b2":
            sent(*p)

    for c in range(PARTS):
        arrived(*plans["b2", c])
        for i in range(PART_HEADS):
            h = c * PART_HEADS + i
            state = b2_recv[c, :, part(i), :].reshape(n, n).astype(jnp.bfloat16)
            gk_ref[:, cols(h)] = (
                gki_ref[h] + kd_ref[h] * dot(v_ref[:, cols(h)], state, 1, 1)
            ).astype(jnp.bfloat16)
            gv_ref[:, cols(h)] = (gvi_ref[h] + dot(ks_ref[h], state, 1, 0)).astype(jnp.bfloat16)
    stores[2].start()
    stores[3].start()
    for c in range(PARTS):
        sent(*plans["b2", c])
    for c in stores:
        c.wait()


def body(queries, keys, values, log_decay, gain, grad_out):
    n = HEAD_DIM
    shape = queries.shape
    f32, bf16 = jnp.float32, jnp.bfloat16
    anywhere = pl.BlockSpec(memory_space=pl.ANY)
    vmem = pl.BlockSpec(memory_space=pltpu.VMEM)
    full = pltpu.VMEM(shape, bf16)
    wide = pltpu.VMEM((LOCAL_HEADS, n, n), f32)
    half = pltpu.VMEM((LOCAL_HEADS, n, n), bf16)

    def slots(rows):
        return [pltpu.VMEM((PARTS, 8, rows, n), f32)] * 2

    return tuple(
        pl.pallas_call(
            kernel,
            out_shape=[jax.ShapeDtypeStruct(shape, bf16)] * 4,
            in_specs=[anywhere, anywhere, anywhere, vmem, vmem, anywhere],
            out_specs=[anywhere] * 4,
            scratch_shapes=[
                *[full] * 8,
                wide, wide, wide, half, half, half, wide, wide, half, half, wide, wide,
                *slots(ROWS + 8), *slots(SUB + 8), *slots(SUB), *slots(ROWS),
                *slots(ROWS), *slots(SUB), *slots(SUB), *slots(ROWS),
                pltpu.VMEM((8, n), f32), pltpu.VMEM((8, 8, n), f32),
                pltpu.SemaphoreType.DMA((4,)), pltpu.SemaphoreType.DMA((4,)),
                pltpu.SemaphoreType.DMA((8 * PARTS + 1, 7)), pltpu.SemaphoreType.DMA((8 * PARTS + 1, 7)),
            ],
            compiler_params=pltpu.CompilerParams(
                collective_id=0, has_side_effects=True, vmem_limit_bytes=40 * 2**20
            ),
            cost_estimate=pl.CostEstimate(flops=600_000_000, bytes_accessed=3_000_000, transcendentals=400_000),
        )(queries, keys, values, log_decay, gain.reshape(1, -1), grad_out)
    )


def solution(mesh):
    finer = Mesh(mesh.devices.reshape(8, 2, 4, mesh.shape["head"]), AXES)
    ctx = ("zh", "zl", "x")
    both = P(ctx, "head")
    return jax.shard_map(
        body,
        mesh=finer,
        in_specs=(both, both, both, both, P("head"), both),
        out_specs=(both,) * 4,
        check_vma=False,
    )
```

```python
import functools

import jax
import jax.numpy as jnp
from jax import lax
from jax.experimental import pallas as pl
from jax.experimental.pallas import tpu as pltpu
from jax.sharding import Mesh
from jax.sharding import PartitionSpec as P

HEADS = 64
HEAD_DIM = 128
GROUP = 8
GROUPS = 8
PARTS = 2
LOCAL_HEADS = 8
PART_HEADS = LOCAL_HEADS // PARTS
SLICE = HEAD_DIM // GROUP
ROWS = PART_HEADS * SLICE
VMEM_LIMIT = 56 * 2**20
SUB = ROWS // GROUPS
FAR_FIRST = (4, 3, 5, 2, 6, 1, 7)
AXES = ("zh", "zl", "x", "head")
MESH = pl.DeviceIdType.MESH

epsilon = 1e-06


def dot(a, b, ca, cb, precision=None):
    return lax.dot_general(
        a, b, (((ca,), (cb,)), ((), ())), preferred_element_type=jnp.float32, precision=precision
    )


def kernel(
    q_hbm, k_hbm, v_hbm, log_ref, gain_ref, g_hbm,
    normed_out, gq_out, gk_out, gv_out,
    q_ref, k_ref, v_ref, g_ref, n_ref, gq_ref, gk_ref, gv_ref,
    decay_ref, kd_ref, qd_ref, ks_ref, qst_ref, w_ref, att_ref, sg_ref, ga_ref, s_ref, gki_ref, gvi_ref,
    a_send, a_recv, z_send, z_recv, y_send, y_recv, b_send, b_recv,
    a2_send, a2_recv, z2_send, z2_recv, y2_send, y2_recv, b2_send, b2_recv,
    h_send, h_recv, in_sem, out_sem, send_sem, recv_sem, near_sem, far_sem,
):
    zh, zl, x, head = (lax.axis_index(a) for a in AXES)
    me = zl * 4 + x

    def group_device(j):
        return (zh, lax.div(j, 4), lax.rem(j, 4), head)

    def groups_device(j):
        return (j, zl, x, head)

    def head_device(j):
        return (zh, zl, x, j)

    def copies(src, dst, mine, device, slot, arriving):
        for k in FAR_FIRST:
            j = lax.rem(mine + (8 - k if arriving else k), 8)
            yield pltpu.make_async_remote_copy(
                src_ref=src(j),
                dst_ref=dst(j if arriving else mine),
                send_sem=send_sem.at[slot, k - 1],
                recv_sem=recv_sem.at[slot, k - 1],
                device_id=device(j),
                device_id_type=MESH,
            )

    def exchange(src, dst, mine, device, slot):
        for c in copies(src, dst, mine, device, slot, False):
            c.start()

    def arrived(src, dst, mine, device, slot):
        for c in copies(src, dst, mine, device, slot, True):
            c.wait_recv()

    def sent(src, dst, mine, device, slot):
        for c in copies(src, dst, mine, device, slot, False):
            c.wait_send()

    barrier = pltpu.get_barrier_semaphore()
    def tell(sem, mine, device, offsets):
        for k in offsets:
            pl.semaphore_signal(
                sem, inc=1, device_id=device(lax.rem(mine + k, 8)), device_id_type=MESH
            )

    tell(barrier, me, group_device, FAR_FIRST)
    tell(barrier, head, head_device, FAR_FIRST)
    tell(barrier, zh, groups_device, (1, 7))
    loads = [
        pltpu.make_async_copy(a, b, in_sem.at[i])
        for i, (a, b) in enumerate(((k_hbm, k_ref), (v_hbm, v_ref), (q_hbm, q_ref), (g_hbm, g_ref)))
    ]
    for c in loads:
        c.start()

    def cols(h):
        return slice(h * HEAD_DIM, (h + 1) * HEAD_DIM)

    n = HEAD_DIM
    row = lax.broadcasted_iota(jnp.int32, (n, n), 0)
    col = lax.broadcasted_iota(jnp.int32, (n, n), 1)
    upto = jnp.where(row <= col, 1.0, 0.0).astype(jnp.float32)
    cum = dot(log_ref[...], upto, 1, 0, lax.Precision.HIGHEST)
    last = jnp.broadcast_to(cum[:, n - 1 :], (LOCAL_HEADS, n))
    block_decay = jnp.exp(last)

    def across(r):
        return jnp.broadcast_to(r, (n, n))

    def at(ref, c):
        return lambda j: ref.at[c, j]

    plans = {}
    slot = 0
    for name, (s, r, mine, device) in {
        "a": (a_send, a_recv, me, group_device),
        "z": (z_send, z_recv, zh, groups_device),
        "y": (y_send, y_recv, zh, groups_device),
        "b": (b_send, b_recv, me, group_device),
        "a2": (a2_send, a2_recv, me, group_device),
        "z2": (z2_send, z2_recv, zh, groups_device),
        "y2": (y2_send, y2_recv, zh, groups_device),
        "b2": (b2_send, b2_recv, me, group_device),
    }.items():
        for c in range(PARTS):
            plans[name, c] = (at(s, c), at(r, c), mine, device, slot)
            slot += 1
    plans["h"] = (lambda j: h_send, lambda j: h_recv.at[j], head, head_device, slot)

    def go(name, c, s, r, mine):
        r[c, mine] = s[c, mine]
        exchange(*plans[name, c])

    loads[0].wait()
    loads[1].wait()
    for c in range(PARTS):
        for i in range(PART_HEADS):
            h = c * PART_HEADS + i
            cum_col = across(cum[h : h + 1]).T
            key_decay = jnp.exp(last[h : h + 1] - cum_col)
            kd_ref[h] = key_decay
            qd_ref[h] = jnp.exp(cum_col)
            ks = (key_decay * k_ref[:, cols(h)].astype(jnp.float32)).astype(jnp.bfloat16)
            ks_ref[h] = ks
            decay_ref[h] = jnp.where(
                row >= col, jnp.exp(jnp.minimum(cum_col - across(cum[h : h + 1]), 0.0)), 0.0
            )
            state = dot(ks, v_ref[:, cols(h)], 0, 0)
            a_send[c, :, i * SLICE : (i + 1) * SLICE, :] = state.reshape(GROUP, SLICE, n)
        a_send[c, :, ROWS:, :] = jnp.broadcast_to(block_decay[None], (GROUP, LOCAL_HEADS, n))
        if c == 0:
            pl.semaphore_wait(barrier, 16)
            tell(near_sem, zh, groups_device, (1, 7))
        go("a", c, a_send, a_recv, me)

    pl.semaphore_wait(near_sem, 2)
    tell(far_sem, zh, groups_device, (2, 6))
    loads[2].wait()
    loads[3].wait()

    def forward_local(h):
        q = q_ref[:, cols(h)]
        w = (dot(q, k_ref[:, cols(h)], 1, 1) * decay_ref[h]).astype(jnp.bfloat16)
        w_ref[h] = w
        att_ref[h] = dot(w, v_ref[:, cols(h)], 1, 0)

    def forward_more(h):
        qst_ref[h] = (qd_ref[h] * q_ref[:, cols(h)].astype(jnp.float32)).T.astype(jnp.bfloat16)
        sg_ref[h] = g_ref[:, cols(h)].astype(jnp.float32) * gain_ref[:, cols(h)]

    for h in range(LOCAL_HEADS):
        forward_local(h)

    def decay_of(c, j, i):
        h = c * PART_HEADS + i
        return a_recv[c, j, ROWS + h : ROWS + h + 1, :]

    def part(i):
        return slice(i * SLICE, (i + 1) * SLICE)

    forward = range(8)
    backward = range(7, -1, -1)

    pl.semaphore_wait(far_sem, 2)
    for c in range(PARTS):
        arrived(*plans["a", c])
        folded, decays = [], []
        for i in range(PART_HEADS):
            total = a_recv[c, 0, part(i), :]
            decay = decay_of(c, 0, i)
            for j in range(1, GROUP):
                d = decay_of(c, j, i)
                total = d * total + a_recv[c, j, part(i), :]
                decay = d * decay
            folded.append(total)
            decays.append(jnp.broadcast_to(decay, (SLICE * 8 // SUB, n)))
        z_send[c, :, :SUB, :] = jnp.concatenate(folded, axis=0).reshape(GROUPS, SUB, n)
        z_send[c, :, SUB:, :] = jnp.concatenate(decays, axis=0).reshape(GROUPS, 8, n)
        go("z", c, z_send, z_recv, zh)

    for h in range(LOCAL_HEADS):
        forward_more(h)

    for c in range(PARTS):
        arrived(*plans["z", c])
        state = jnp.zeros((SUB, n), jnp.float32)
        for g in forward:
            y_send[c, g] = state
            state = z_recv[c, g, SUB : SUB + 1, :] * state + z_recv[c, g, :SUB, :]
        go("y", c, y_send, y_recv, zh)

    for c in range(PARTS):
        arrived(*plans["y", c])
        entering = y_recv[c].reshape(ROWS, n)
        for i in range(PART_HEADS):
            state = entering[part(i)]
            for j in forward:
                b_send[c, j, part(i), :] = state
                state = decay_of(c, j, i) * state + a_recv[c, j, part(i), :]
        go("b", c, b_send, b_recv, me)

    squares = jnp.zeros((n, n), jnp.float32)
    products = jnp.zeros((n, n), jnp.float32)
    for c in range(PARTS):
        arrived(*plans["b", c])
        for i in range(PART_HEADS):
            h = c * PART_HEADS + i
            state = b_recv[c, :, part(i), :].reshape(n, n).astype(jnp.bfloat16)
            s_ref[h] = state
            att = att_ref[h] + qd_ref[h] * dot(q_ref[:, cols(h)], state, 1, 0)
            att_ref[h] = att
            squares += att * att
            products += sg_ref[h] * att

    sums = jnp.where(
        lax.broadcasted_iota(jnp.int32, (8, n), 0) == 0,
        jnp.sum(squares.T, axis=0, keepdims=True),
        jnp.sum(products.T, axis=0, keepdims=True),
    )
    h_send[...] = sums
    h_recv[head] = sums
    exchange(*plans["h"])
    arrived(*plans["h"])
    sums = h_recv[0]
    for j in range(1, 8):
        sums += h_recv[j]
    width = HEADS * HEAD_DIM
    inverse_row = lax.rsqrt(sums[0:1] / width + epsilon)
    factor_row = inverse_row * inverse_row * inverse_row * sums[1:2] / width
    inverse = across(inverse_row).T
    factor = across(factor_row).T

    for c in range(PARTS):
        for i in range(PART_HEADS):
            h = c * PART_HEADS + i
            ga = (inverse * sg_ref[h] - att_ref[h] * factor).astype(jnp.bfloat16)
            ga_ref[h] = ga
            a2_send[c, :, part(i), :] = dot(qst_ref[h], ga, 1, 0).reshape(GROUP, SLICE, n)
        go("a2", c, a2_send, a2_recv, me)

    def backward_local(h):
        ga = ga_ref[h]
        gs = (dot(ga, v_ref[:, cols(h)], 1, 1) * decay_ref[h]).astype(jnp.bfloat16)
        gq_ref[:, cols(h)] = (
            dot(gs, k_ref[:, cols(h)], 1, 0) + qd_ref[h] * dot(ga, s_ref[h], 1, 1)
        ).astype(jnp.bfloat16)
        gki_ref[h] = dot(gs, q_ref[:, cols(h)], 0, 0)
        gvi_ref[h] = dot(w_ref[h], ga, 0, 0)
        n_ref[:, cols(h)] = (att_ref[h] * inverse * gain_ref[:, cols(h)]).astype(jnp.bfloat16)

    for h in range(PART_HEADS):
        backward_local(h)

    for c in range(PARTS):
        arrived(*plans["a2", c])
        folded = []
        for i in range(PART_HEADS):
            total = a2_recv[c, GROUP - 1, part(i), :]
            for j in range(GROUP - 2, -1, -1):
                total = decay_of(c, j, i) * total + a2_recv[c, j, part(i), :]
            folded.append(total)
        z2_send[c] = jnp.concatenate(folded, axis=0).reshape(GROUPS, SUB, n)
        go("z2", c, z2_send, z2_recv, zh)

    for h in range(PART_HEADS, LOCAL_HEADS):
        backward_local(h)
    stores = [
        pltpu.make_async_copy(a, b, out_sem.at[i])
        for i, (a, b) in enumerate(
            ((n_ref, normed_out), (gq_ref, gq_out), (gk_ref, gk_out), (gv_ref, gv_out))
        )
    ]
    stores[0].start()
    stores[1].start()

    for c in range(PARTS):
        arrived(*plans["z2", c])
        state = jnp.zeros((SUB, n), jnp.float32)
        for g in backward:
            y2_send[c, g] = state
            state = z_recv[c, g, SUB : SUB + 1, :] * state + z2_recv[c, g]
        go("y2", c, y2_send, y2_recv, zh)

    for c in range(PARTS):
        arrived(*plans["y2", c])
        later = y2_recv[c].reshape(ROWS, n)
        for i in range(PART_HEADS):
            state = later[part(i)]
            for j in backward:
                b2_send[c, j, part(i), :] = state
                state = decay_of(c, j, i) * state + a2_recv[c, j, part(i), :]
        go("b2", c, b2_send, b2_recv, me)

    for key, p in plans.items():
        if key[0] != "b2":
            sent(*p)

    for c in range(PARTS):
        arrived(*plans["b2", c])
        for i in range(PART_HEADS):
            h = c * PART_HEADS + i
            state = b2_recv[c, :, part(i), :].reshape(n, n).astype(jnp.bfloat16)
            gk_ref[:, cols(h)] = (
                gki_ref[h] + kd_ref[h] * dot(v_ref[:, cols(h)], state, 1, 1)
            ).astype(jnp.bfloat16)
            gv_ref[:, cols(h)] = (gvi_ref[h] + dot(ks_ref[h], state, 1, 0)).astype(jnp.bfloat16)
    stores[2].start()
    stores[3].start()
    for c in range(PARTS):
        sent(*plans["b2", c])
    for c in stores:
        c.wait()


def write_out(*refs):
    held, load_sem, store_sem = refs[8:]
    loads = [pltpu.make_async_copy(refs[i], held.at[i], load_sem.at[i]) for i in range(4)]
    stores = [pltpu.make_async_copy(held.at[i], refs[4 + i], store_sem.at[i]) for i in range(4)]
    for c in loads:
        c.start()
    for load, store in zip(loads, stores):
        load.wait()
        store.start()
    for c in stores:
        c.wait()


def body(queries, keys, values, log_decay, gain, grad_out):
    n = HEAD_DIM
    shape = queries.shape
    f32, bf16 = jnp.float32, jnp.bfloat16
    hbm = pl.BlockSpec(memory_space=pltpu.HBM)
    vmem = pl.BlockSpec(memory_space=pltpu.VMEM)
    full = pltpu.VMEM(shape, bf16)
    wide = pltpu.VMEM((LOCAL_HEADS, n, n), f32)
    half = pltpu.VMEM((LOCAL_HEADS, n, n), bf16)

    def slots(rows):
        return [pltpu.VMEM((PARTS, 8, rows, n), f32)] * 2

    made = pl.pallas_call(
            kernel,
            out_shape=[jax.ShapeDtypeStruct(shape, bf16)] * 4,
            in_specs=[hbm, hbm, hbm, vmem, vmem, hbm],
            out_specs=[hbm] * 4,
            scratch_shapes=[
                *[full] * 8,
                wide, wide, wide, half, half, half, wide, wide, half, half, wide, wide,
                *slots(ROWS + 8), *slots(SUB + 8), *slots(SUB), *slots(ROWS),
                *slots(ROWS), *slots(SUB), *slots(SUB), *slots(ROWS),
                pltpu.VMEM((8, n), f32), pltpu.VMEM((8, 8, n), f32),
                pltpu.SemaphoreType.DMA((4,)), pltpu.SemaphoreType.DMA((4,)),
                pltpu.SemaphoreType.DMA((8 * PARTS + 1, 7)), pltpu.SemaphoreType.DMA((8 * PARTS + 1, 7)),
                pltpu.SemaphoreType.REGULAR, pltpu.SemaphoreType.REGULAR,
            ],
            compiler_params=pltpu.CompilerParams(
                collective_id=0, has_side_effects=True, vmem_limit_bytes=VMEM_LIMIT
            ),
            cost_estimate=pl.CostEstimate(flops=600_000_000, bytes_accessed=3_000_000, transcendentals=400_000),
        )(queries, keys, values, log_decay.T, gain.reshape(1, -1), grad_out)
    return tuple(
        pl.pallas_call(
            write_out,
            out_shape=[jax.ShapeDtypeStruct(shape, bf16)] * 4,
            in_specs=[hbm] * 4,
            out_specs=[hbm] * 4,
            scratch_shapes=[
                pltpu.VMEM((4, *shape), bf16),
                pltpu.SemaphoreType.DMA((4,)),
                pltpu.SemaphoreType.DMA((4,)),
            ],
            compiler_params=pltpu.CompilerParams(vmem_limit_bytes=VMEM_LIMIT),
        )(*made)
    )


def solution(mesh):
    finer = Mesh(mesh.devices.reshape(8, 2, 4, mesh.shape["head"]), AXES)
    ctx = ("zh", "zl", "x")
    both = P(ctx, "head")
    return jax.shard_map(
        body,
        mesh=finer,
        in_specs=(both, both, both, both, P("head"), both),
        out_specs=(both,) * 4,
        check_vma=False,
    )
```

```python
import functools

import jax
import jax.numpy as jnp
from jax import lax
from jax.experimental import pallas as pl
from jax.experimental.pallas import tpu as pltpu
from jax.sharding import Mesh
from jax.sharding import PartitionSpec as P

HEADS = 64
HEAD_DIM = 128
GROUP = 8
GROUPS = 8
PARTS = 2
LOCAL_HEADS = 8
PART_HEADS = LOCAL_HEADS // PARTS
SLICE = HEAD_DIM // GROUP
ROWS = PART_HEADS * SLICE
VMEM_LIMIT = 54016 * 1024
SUB = ROWS // GROUPS
FAR_FIRST = (4, 3, 5, 2, 6, 1, 7)
AXES = ("zh", "zl", "x", "head")
MESH = pl.DeviceIdType.MESH

epsilon = 1e-06


def dot(a, b, ca, cb, precision=None):
    return lax.dot_general(
        a, b, (((ca,), (cb,)), ((), ())), preferred_element_type=jnp.float32, precision=precision
    )


def kernel(
    q_hbm, k_hbm, v_hbm, log_ref, gain_ref, g_hbm,
    n_ref, gq_ref, gk_ref, gv_ref,
    q_ref, k_ref, v_ref, g_ref,
    cum_ref, decay_ref, kd_ref, qd_ref, ks_ref, qst_ref, w_ref, att_ref, sg_ref, ga_ref, s_ref, gki_ref, gvi_ref,
    a_send, a_recv, z_send, z_recv, y_send, y_recv, b_send, b_recv,
    a2_send, a2_recv, z2_send, z2_recv, y2_send, y2_recv, b2_send, b2_recv,
    h_send, h_recv, in_sem, send_sem, recv_sem, near_sem, far_sem,
):
    zh, zl, x, head = (lax.axis_index(a) for a in AXES)
    me = zl * 4 + x

    def group_device(j):
        return (zh, lax.div(j, 4), lax.rem(j, 4), head)

    def groups_device(j):
        return (j, zl, x, head)

    def head_device(j):
        return (zh, zl, x, j)

    def copies(src, dst, mine, device, slot, arriving):
        for k in FAR_FIRST:
            j = lax.rem(mine + (8 - k if arriving else k), 8)
            yield pltpu.make_async_remote_copy(
                src_ref=src(j),
                dst_ref=dst(j if arriving else mine),
                send_sem=send_sem.at[slot, k - 1],
                recv_sem=recv_sem.at[slot, k - 1],
                device_id=device(j),
                device_id_type=MESH,
            )

    def exchange(src, dst, mine, device, slot):
        for c in copies(src, dst, mine, device, slot, False):
            c.start()

    def arrived(src, dst, mine, device, slot):
        for c in copies(src, dst, mine, device, slot, True):
            c.wait_recv()

    def sent(src, dst, mine, device, slot):
        for c in copies(src, dst, mine, device, slot, False):
            c.wait_send()

    barrier = pltpu.get_barrier_semaphore()
    def tell(sem, mine, device, offsets):
        for k in offsets:
            pl.semaphore_signal(
                sem, inc=1, device_id=device(lax.rem(mine + k, 8)), device_id_type=MESH
            )

    tell(barrier, me, group_device, FAR_FIRST)
    tell(barrier, head, head_device, FAR_FIRST)
    tell(barrier, zh, groups_device, (1, 7))
    loads = [
        pltpu.make_async_copy(a, b, in_sem.at[i])
        for i, (a, b) in enumerate(((k_hbm, k_ref), (v_hbm, v_ref), (q_hbm, q_ref), (g_hbm, g_ref)))
    ]
    for c in loads:
        c.start()

    def cols(h):
        return slice(h * HEAD_DIM, (h + 1) * HEAD_DIM)

    n = HEAD_DIM
    row = lax.broadcasted_iota(jnp.int32, (n, n), 0)
    col = lax.broadcasted_iota(jnp.int32, (n, n), 1)
    upto = jnp.where(row <= col, 1.0, 0.0).astype(jnp.float32)
    cum = dot(log_ref[...], upto, 1, 0, lax.Precision.HIGHEST)
    last = jnp.broadcast_to(cum[:, n - 1 :], (LOCAL_HEADS, n))
    block_decay = jnp.exp(last)

    def across(r):
        return jnp.broadcast_to(r, (n, n))

    def at(ref, c):
        return lambda j: ref.at[c, j]

    plans = {}
    slot = 0
    for name, (s, r, mine, device) in {
        "a": (a_send, a_recv, me, group_device),
        "z": (z_send, z_recv, zh, groups_device),
        "y": (y_send, y_recv, zh, groups_device),
        "b": (b_send, b_recv, me, group_device),
        "a2": (a2_send, a2_recv, me, group_device),
        "z2": (z2_send, z2_recv, zh, groups_device),
        "y2": (y2_send, y2_recv, zh, groups_device),
        "b2": (b2_send, b2_recv, me, group_device),
    }.items():
        for c in range(PARTS):
            plans[name, c] = (at(s, c), at(r, c), mine, device, slot)
            slot += 1
    plans["h"] = (lambda j: h_send, lambda j: h_recv.at[j], head, head_device, slot)

    def go(name, c, s, r, mine):
        r[c, mine] = s[c, mine]
        exchange(*plans[name, c])

    loads[0].wait()
    loads[1].wait()
    for c in range(PARTS):
        for i in range(PART_HEADS):
            h = c * PART_HEADS + i
            cum_col = across(cum[h : h + 1]).T
            key_decay = jnp.exp(last[h : h + 1] - cum_col)
            kd_ref[h] = key_decay
            cum_ref[h] = cum_col
            ks = (key_decay * k_ref[:, cols(h)].astype(jnp.float32)).astype(jnp.bfloat16)
            ks_ref[h] = ks
            state = dot(ks, v_ref[:, cols(h)], 0, 0)
            a_send[c, :, i * SLICE : (i + 1) * SLICE, :] = state.reshape(GROUP, SLICE, n)
        a_send[c, :, ROWS:, :] = jnp.broadcast_to(block_decay[None], (GROUP, LOCAL_HEADS, n))
        if c == 0:
            pl.semaphore_wait(barrier, 16)
            tell(near_sem, zh, groups_device, (1, 7))
        go("a", c, a_send, a_recv, me)

    pl.semaphore_wait(near_sem, 2)
    tell(far_sem, zh, groups_device, (2, 6))
    loads[2].wait()
    loads[3].wait()

    def forward_local(h):
        q = q_ref[:, cols(h)]
        cum_col = cum_ref[h]
        qd_ref[h] = jnp.exp(cum_col)
        decay_ref[h] = jnp.where(
            row >= col, jnp.exp(jnp.minimum(cum_col - across(cum[h : h + 1]), 0.0)), 0.0
        )
        w = (dot(q, k_ref[:, cols(h)], 1, 1) * decay_ref[h]).astype(jnp.bfloat16)
        w_ref[h] = w
        att_ref[h] = dot(w, v_ref[:, cols(h)], 1, 0)

    def forward_more(h):
        qst_ref[h] = (qd_ref[h] * q_ref[:, cols(h)].astype(jnp.float32)).T.astype(jnp.bfloat16)
        sg_ref[h] = g_ref[:, cols(h)].astype(jnp.float32) * gain_ref[:, cols(h)]

    for h in range(LOCAL_HEADS):
        forward_local(h)

    def decay_of(c, j, i):
        h = c * PART_HEADS + i
        return a_recv[c, j, ROWS + h : ROWS + h + 1, :]

    def part(i):
        return slice(i * SLICE, (i + 1) * SLICE)

    forward = range(8)
    backward = range(7, -1, -1)

    pl.semaphore_wait(far_sem, 2)
    for c in range(PARTS):
        arrived(*plans["a", c])
        folded, decays = [], []
        for i in range(PART_HEADS):
            total = a_recv[c, 0, part(i), :]
            decay = decay_of(c, 0, i)
            for j in range(1, GROUP):
                d = decay_of(c, j, i)
                total = d * total + a_recv[c, j, part(i), :]
                decay = d * decay
            folded.append(total)
            decays.append(jnp.broadcast_to(decay, (SLICE * 8 // SUB, n)))
        z_send[c, :, :SUB, :] = jnp.concatenate(folded, axis=0).reshape(GROUPS, SUB, n)
        z_send[c, :, SUB:, :] = jnp.concatenate(decays, axis=0).reshape(GROUPS, 8, n)
        go("z", c, z_send, z_recv, zh)

    for h in range(LOCAL_HEADS):
        forward_more(h)

    for c in range(PARTS):
        arrived(*plans["z", c])
        state = jnp.zeros((SUB, n), jnp.float32)
        for g in forward:
            y_send[c, g] = state
            state = z_recv[c, g, SUB : SUB + 1, :] * state + z_recv[c, g, :SUB, :]
        go("y", c, y_send, y_recv, zh)

    for c in range(PARTS):
        arrived(*plans["y", c])
        entering = y_recv[c].reshape(ROWS, n)
        for i in range(PART_HEADS):
            state = entering[part(i)]
            for j in forward:
                b_send[c, j, part(i), :] = state
                state = decay_of(c, j, i) * state + a_recv[c, j, part(i), :]
        go("b", c, b_send, b_recv, me)

    squares = jnp.zeros((n, n), jnp.float32)
    products = jnp.zeros((n, n), jnp.float32)
    for c in range(PARTS):
        arrived(*plans["b", c])
        for i in range(PART_HEADS):
            h = c * PART_HEADS + i
            state = b_recv[c, :, part(i), :].reshape(n, n).astype(jnp.bfloat16)
            s_ref[h] = state
            att = att_ref[h] + qd_ref[h] * dot(q_ref[:, cols(h)], state, 1, 0)
            att_ref[h] = att
            squares += att * att
            products += sg_ref[h] * att

    sums = jnp.where(
        lax.broadcasted_iota(jnp.int32, (8, n), 0) == 0,
        jnp.sum(squares.T, axis=0, keepdims=True),
        jnp.sum(products.T, axis=0, keepdims=True),
    )
    h_send[...] = sums
    h_recv[head] = sums
    exchange(*plans["h"])
    arrived(*plans["h"])
    sums = h_recv[0]
    for j in range(1, 8):
        sums += h_recv[j]
    width = HEADS * HEAD_DIM
    inverse_row = lax.rsqrt(sums[0:1] / width + epsilon)
    factor_row = inverse_row * inverse_row * inverse_row * sums[1:2] / width
    inverse = across(inverse_row).T
    factor = across(factor_row).T

    for c in range(PARTS):
        for i in range(PART_HEADS):
            h = c * PART_HEADS + i
            ga = (inverse * sg_ref[h] - att_ref[h] * factor).astype(jnp.bfloat16)
            ga_ref[h] = ga
            a2_send[c, :, part(i), :] = dot(qst_ref[h], ga, 1, 0).reshape(GROUP, SLICE, n)
        go("a2", c, a2_send, a2_recv, me)

    def backward_local(h):
        ga = ga_ref[h]
        gs = (dot(ga, v_ref[:, cols(h)], 1, 1) * decay_ref[h]).astype(jnp.bfloat16)
        gq_ref[:, cols(h)] = (
            dot(gs, k_ref[:, cols(h)], 1, 0) + qd_ref[h] * dot(ga, s_ref[h], 1, 1)
        ).astype(jnp.bfloat16)
        gki_ref[h] = dot(gs, q_ref[:, cols(h)], 0, 0)
        gvi_ref[h] = dot(w_ref[h], ga, 0, 0)
        n_ref[:, cols(h)] = (att_ref[h] * inverse * gain_ref[:, cols(h)]).astype(jnp.bfloat16)

    for h in range(PART_HEADS):
        backward_local(h)

    for c in range(PARTS):
        arrived(*plans["a2", c])
        folded = []
        for i in range(PART_HEADS):
            total = a2_recv[c, GROUP - 1, part(i), :]
            for j in range(GROUP - 2, -1, -1):
                total = decay_of(c, j, i) * total + a2_recv[c, j, part(i), :]
            folded.append(total)
        z2_send[c] = jnp.concatenate(folded, axis=0).reshape(GROUPS, SUB, n)
        go("z2", c, z2_send, z2_recv, zh)

    for h in range(PART_HEADS, LOCAL_HEADS):
        backward_local(h)
    for c in range(PARTS):
        arrived(*plans["z2", c])
        state = jnp.zeros((SUB, n), jnp.float32)
        for g in backward:
            y2_send[c, g] = state
            state = z_recv[c, g, SUB : SUB + 1, :] * state + z2_recv[c, g]
        go("y2", c, y2_send, y2_recv, zh)

    for c in range(PARTS):
        arrived(*plans["y2", c])
        later = y2_recv[c].reshape(ROWS, n)
        for i in range(PART_HEADS):
            state = later[part(i)]
            for j in backward:
                b2_send[c, j, part(i), :] = state
                state = decay_of(c, j, i) * state + a2_recv[c, j, part(i), :]
        go("b2", c, b2_send, b2_recv, me)

    for key, p in plans.items():
        if key[0] != "b2":
            sent(*p)

    for c in range(PARTS):
        arrived(*plans["b2", c])
        for i in range(PART_HEADS):
            h = c * PART_HEADS + i
            state = b2_recv[c, :, part(i), :].reshape(n, n).astype(jnp.bfloat16)
            gk_ref[:, cols(h)] = (
                gki_ref[h] + kd_ref[h] * dot(v_ref[:, cols(h)], state, 1, 1)
            ).astype(jnp.bfloat16)
            gv_ref[:, cols(h)] = (gvi_ref[h] + dot(ks_ref[h], state, 1, 0)).astype(jnp.bfloat16)
    for c in range(PARTS):
        sent(*plans["b2", c])


def write_out(*refs):
    sem = refs[8]
    stores = [pltpu.make_async_copy(refs[i], refs[4 + i], sem.at[i]) for i in range(4)]
    for c in stores:
        c.start()
    for c in stores:
        c.wait()


def body(queries, keys, values, log_decay, gain, grad_out):
    n = HEAD_DIM
    shape = queries.shape
    f32, bf16 = jnp.float32, jnp.bfloat16
    hbm = pl.BlockSpec(memory_space=pltpu.HBM)
    vmem = pl.BlockSpec(memory_space=pltpu.VMEM)
    full = pltpu.VMEM(shape, bf16)
    wide = pltpu.VMEM((LOCAL_HEADS, n, n), f32)
    half = pltpu.VMEM((LOCAL_HEADS, n, n), bf16)

    def slots(rows):
        return [pltpu.VMEM((PARTS, 8, rows, n), f32)] * 2

    made = pl.pallas_call(
            kernel,
            out_shape=[jax.ShapeDtypeStruct(shape, bf16)] * 4,
            in_specs=[hbm, hbm, hbm, vmem, vmem, hbm],
            out_specs=[vmem] * 4,
            scratch_shapes=[
                *[full] * 4,
                wide, wide, wide, wide, half, half, half, wide, wide, half, half, wide, wide,
                *slots(ROWS + 8), *slots(SUB + 8), *slots(SUB), *slots(ROWS),
                *slots(ROWS), *slots(SUB), *slots(SUB), *slots(ROWS),
                pltpu.VMEM((8, n), f32), pltpu.VMEM((8, 8, n), f32),
                pltpu.SemaphoreType.DMA((4,)),
                pltpu.SemaphoreType.DMA((8 * PARTS + 1, 7)), pltpu.SemaphoreType.DMA((8 * PARTS + 1, 7)),
                pltpu.SemaphoreType.REGULAR, pltpu.SemaphoreType.REGULAR,
            ],
            compiler_params=pltpu.CompilerParams(
                collective_id=0, has_side_effects=True, vmem_limit_bytes=VMEM_LIMIT
            ),
            cost_estimate=pl.CostEstimate(flops=600_000_000, bytes_accessed=3_000_000, transcendentals=400_000),
        )(queries, keys, values, log_decay.T, gain.reshape(1, -1), grad_out)
    return tuple(
        pl.pallas_call(
            write_out,
            out_shape=[jax.ShapeDtypeStruct(shape, bf16)] * 4,
            in_specs=[pl.BlockSpec(memory_space=pl.ANY)] * 4,
            out_specs=[hbm] * 4,
            scratch_shapes=[pltpu.SemaphoreType.DMA((4,))],
            compiler_params=pltpu.CompilerParams(vmem_limit_bytes=16 * 2**20),
        )(*made)
    )


def solution(mesh):
    finer = Mesh(mesh.devices.reshape(8, 2, 4, mesh.shape["head"]), AXES)
    ctx = ("zh", "zl", "x")
    both = P(ctx, "head")
    return jax.shard_map(
        body,
        mesh=finer,
        in_specs=(both, both, both, both, P("head"), both),
        out_specs=(both,) * 4,
        check_vma=False,
    )
```

```python
import functools

import jax
import jax.numpy as jnp
from jax import lax
from jax.experimental import pallas as pl
from jax.experimental.pallas import tpu as pltpu
from jax.sharding import Mesh
from jax.sharding import PartitionSpec as P

HEADS = 64
HEAD_DIM = 128
GROUP = 8
GROUPS = 8
PARTS = 2
LOCAL_HEADS = 8
PART_HEADS = LOCAL_HEADS // PARTS
SLICE = HEAD_DIM // GROUP
ROWS = PART_HEADS * SLICE
VMEM_LIMIT = 54016 * 1024
SUB = ROWS // GROUPS
FAR_FIRST = (4, 3, 5, 2, 6, 1, 7)
GROUP_FAR_FIRST = (6, 2, 5, 3, 7, 1, 4)
AXES = ("zh", "zl", "x", "head")
MESH = pl.DeviceIdType.MESH

epsilon = 1e-06


def dot(a, b, ca, cb, precision=None):
    return lax.dot_general(
        a, b, (((ca,), (cb,)), ((), ())), preferred_element_type=jnp.float32, precision=precision
    )


def kernel(
    q_hbm, k_hbm, v_hbm, log_ref, gain_ref, g_hbm,
    n_ref, gq_ref, gk_ref, gv_ref,
    q_ref, k_ref, v_ref, g_ref,
    cum_ref, decay_ref, kd_ref, qd_ref, ks_ref, qst_ref, w_ref, att_ref, sg_ref, ga_ref, s_ref, gki_ref, gvi_ref,
    a_send, a_recv, z_send, z_recv, y_send, y_recv, b_send, b_recv,
    a2_send, a2_recv, z2_send, z2_recv, y2_send, y2_recv, b2_send, b2_recv,
    h_send, h_recv, in_sem, send_sem, recv_sem, near_sem, far_sem,
):
    zh, zl, x, head = (lax.axis_index(a) for a in AXES)
    me = zl * 4 + x

    def group_device(j):
        return (zh, lax.div(j, 4), lax.rem(j, 4), head)

    def groups_device(j):
        return (j, zl, x, head)

    def head_device(j):
        return (zh, zl, x, j)

    def copies(src, dst, mine, device, slot, arriving):
        for k in GROUP_FAR_FIRST if device is group_device else FAR_FIRST:
            j = lax.rem(mine + (8 - k if arriving else k), 8)
            yield pltpu.make_async_remote_copy(
                src_ref=src(j),
                dst_ref=dst(j if arriving else mine),
                send_sem=send_sem.at[slot, k - 1],
                recv_sem=recv_sem.at[slot, k - 1],
                device_id=device(j),
                device_id_type=MESH,
            )

    def exchange(src, dst, mine, device, slot):
        for c in copies(src, dst, mine, device, slot, False):
            c.start()

    def arrived(src, dst, mine, device, slot):
        for c in copies(src, dst, mine, device, slot, True):
            c.wait_recv()

    def sent(src, dst, mine, device, slot):
        for c in copies(src, dst, mine, device, slot, False):
            c.wait_send()

    barrier = pltpu.get_barrier_semaphore()
    def tell(sem, mine, device, offsets):
        for k in offsets:
            pl.semaphore_signal(
                sem, inc=1, device_id=device(lax.rem(mine + k, 8)), device_id_type=MESH
            )

    tell(barrier, me, group_device, FAR_FIRST)
    tell(barrier, head, head_device, FAR_FIRST)
    tell(barrier, zh, groups_device, (1, 7))
    loads = [
        pltpu.make_async_copy(a, b, in_sem.at[i])
        for i, (a, b) in enumerate(((k_hbm, k_ref), (v_hbm, v_ref), (q_hbm, q_ref), (g_hbm, g_ref)))
    ]
    for c in loads:
        c.start()

    def cols(h):
        return slice(h * HEAD_DIM, (h + 1) * HEAD_DIM)

    n = HEAD_DIM
    row = lax.broadcasted_iota(jnp.int32, (n, n), 0)
    col = lax.broadcasted_iota(jnp.int32, (n, n), 1)
    upto = jnp.where(row <= col, 1.0, 0.0).astype(jnp.float32)
    cum = dot(log_ref[...], upto, 1, 0, lax.Precision.HIGHEST)
    last = jnp.broadcast_to(cum[:, n - 1 :], (LOCAL_HEADS, n))
    block_decay = jnp.exp(last)

    def across(r):
        return jnp.broadcast_to(r, (n, n))

    def at(ref, c):
        return lambda j: ref.at[c, j]

    plans = {}
    slot = 0
    for name, (s, r, mine, device) in {
        "a": (a_send, a_recv, me, group_device),
        "z": (z_send, z_recv, zh, groups_device),
        "y": (y_send, y_recv, zh, groups_device),
        "b": (b_send, b_recv, me, group_device),
        "a2": (a2_send, a2_recv, me, group_device),
        "z2": (z2_send, z2_recv, zh, groups_device),
        "y2": (y2_send, y2_recv, zh, groups_device),
        "b2": (b2_send, b2_recv, me, group_device),
    }.items():
        for c in range(PARTS):
            plans[name, c] = (at(s, c), at(r, c), mine, device, slot)
            slot += 1
    plans["h"] = (lambda j: h_send, lambda j: h_recv.at[j], head, head_device, slot)

    def go(name, c, s, r, mine):
        r[c, mine] = s[c, mine]
        exchange(*plans[name, c])

    loads[0].wait()
    loads[1].wait()
    for c in range(PARTS):
        for i in range(PART_HEADS):
            h = c * PART_HEADS + i
            cum_col = across(cum[h : h + 1]).T
            key_decay = jnp.exp(last[h : h + 1] - cum_col)
            kd_ref[h] = key_decay
            cum_ref[h] = cum_col
            ks = (key_decay * k_ref[:, cols(h)].astype(jnp.float32)).astype(jnp.bfloat16)
            ks_ref[h] = ks
            state = dot(ks, v_ref[:, cols(h)], 0, 0)
            a_send[c, :, i * SLICE : (i + 1) * SLICE, :] = state.reshape(GROUP, SLICE, n)
        a_send[c, :, ROWS:, :] = jnp.broadcast_to(block_decay[None], (GROUP, LOCAL_HEADS, n))
        if c == 0:
            pl.semaphore_wait(barrier, 16)
            tell(near_sem, zh, groups_device, (1, 7))
        go("a", c, a_send, a_recv, me)

    pl.semaphore_wait(near_sem, 2)
    tell(far_sem, zh, groups_device, (2, 6))
    loads[2].wait()
    loads[3].wait()

    def forward_local(h):
        q = q_ref[:, cols(h)]
        cum_col = cum_ref[h]
        qd_ref[h] = jnp.exp(cum_col)
        decay_ref[h] = jnp.where(
            row >= col, jnp.exp(jnp.minimum(cum_col - across(cum[h : h + 1]), 0.0)), 0.0
        )
        w = (dot(q, k_ref[:, cols(h)], 1, 1) * decay_ref[h]).astype(jnp.bfloat16)
        w_ref[h] = w
        att_ref[h] = dot(w, v_ref[:, cols(h)], 1, 0)

    def forward_more(h):
        qst_ref[h] = (qd_ref[h] * q_ref[:, cols(h)].astype(jnp.float32)).T.astype(jnp.bfloat16)
        sg_ref[h] = g_ref[:, cols(h)].astype(jnp.float32) * gain_ref[:, cols(h)]

    for h in range(LOCAL_HEADS):
        forward_local(h)

    def decay_of(c, j, i):
        h = c * PART_HEADS + i
        return a_recv[c, j, ROWS + h : ROWS + h + 1, :]

    def part(i):
        return slice(i * SLICE, (i + 1) * SLICE)

    forward = range(8)
    backward = range(7, -1, -1)

    pl.semaphore_wait(far_sem, 2)
    for c in range(PARTS):
        arrived(*plans["a", c])
        folded, decays = [], []
        for i in range(PART_HEADS):
            total = a_recv[c, 0, part(i), :]
            decay = decay_of(c, 0, i)
            for j in range(1, GROUP):
                d = decay_of(c, j, i)
                total = d * total + a_recv[c, j, part(i), :]
                decay = d * decay
            folded.append(total)
            decays.append(jnp.broadcast_to(decay, (SLICE * 8 // SUB, n)))
        z_send[c, :, :SUB, :] = jnp.concatenate(folded, axis=0).reshape(GROUPS, SUB, n)
        z_send[c, :, SUB:, :] = jnp.concatenate(decays, axis=0).reshape(GROUPS, 8, n)
        go("z", c, z_send, z_recv, zh)

    for h in range(LOCAL_HEADS):
        forward_more(h)

    for c in range(PARTS):
        arrived(*plans["z", c])
        state = jnp.zeros((SUB, n), jnp.float32)
        for g in forward:
            y_send[c, g] = state
            state = z_recv[c, g, SUB : SUB + 1, :] * state + z_recv[c, g, :SUB, :]
        go("y", c, y_send, y_recv, zh)

    for c in range(PARTS):
        arrived(*plans["y", c])
        entering = y_recv[c].reshape(ROWS, n)
        for i in range(PART_HEADS):
            state = entering[part(i)]
            for j in forward:
                b_send[c, j, part(i), :] = state
                state = decay_of(c, j, i) * state + a_recv[c, j, part(i), :]
        go("b", c, b_send, b_recv, me)

    squares = jnp.zeros((n, n), jnp.float32)
    products = jnp.zeros((n, n), jnp.float32)
    for c in range(PARTS):
        arrived(*plans["b", c])
        for i in range(PART_HEADS):
            h = c * PART_HEADS + i
            state = b_recv[c, :, part(i), :].reshape(n, n).astype(jnp.bfloat16)
            s_ref[h] = state
            att = att_ref[h] + qd_ref[h] * dot(q_ref[:, cols(h)], state, 1, 0)
            att_ref[h] = att
            squares += att * att
            products += sg_ref[h] * att

    sums = jnp.where(
        lax.broadcasted_iota(jnp.int32, (8, n), 0) == 0,
        jnp.sum(squares.T, axis=0, keepdims=True),
        jnp.sum(products.T, axis=0, keepdims=True),
    )
    h_send[...] = sums
    h_recv[head] = sums
    exchange(*plans["h"])
    arrived(*plans["h"])
    sums = h_recv[0]
    for j in range(1, 8):
        sums += h_recv[j]
    width = HEADS * HEAD_DIM
    inverse_row = lax.rsqrt(sums[0:1] / width + epsilon)
    factor_row = inverse_row * inverse_row * inverse_row * sums[1:2] / width
    inverse = across(inverse_row).T
    factor = across(factor_row).T

    for c in range(PARTS):
        for i in range(PART_HEADS):
            h = c * PART_HEADS + i
            ga = (inverse * sg_ref[h] - att_ref[h] * factor).astype(jnp.bfloat16)
            ga_ref[h] = ga
            a2_send[c, :, part(i), :] = dot(qst_ref[h], ga, 1, 0).reshape(GROUP, SLICE, n)
        go("a2", c, a2_send, a2_recv, me)

    def backward_local(h):
        ga = ga_ref[h]
        gs = (dot(ga, v_ref[:, cols(h)], 1, 1) * decay_ref[h]).astype(jnp.bfloat16)
        gq_ref[:, cols(h)] = (
            dot(gs, k_ref[:, cols(h)], 1, 0) + qd_ref[h] * dot(ga, s_ref[h], 1, 1)
        ).astype(jnp.bfloat16)
        gki_ref[h] = dot(gs, q_ref[:, cols(h)], 0, 0)
        gvi_ref[h] = dot(w_ref[h], ga, 0, 0)
        n_ref[:, cols(h)] = (att_ref[h] * inverse * gain_ref[:, cols(h)]).astype(jnp.bfloat16)

    for h in range(PART_HEADS):
        backward_local(h)

    for c in range(PARTS):
        arrived(*plans["a2", c])
        folded = []
        for i in range(PART_HEADS):
            total = a2_recv[c, GROUP - 1, part(i), :]
            for j in range(GROUP - 2, -1, -1):
                total = decay_of(c, j, i) * total + a2_recv[c, j, part(i), :]
            folded.append(total)
        z2_send[c] = jnp.concatenate(folded, axis=0).reshape(GROUPS, SUB, n)
        go("z2", c, z2_send, z2_recv, zh)

    for h in range(PART_HEADS, LOCAL_HEADS):
        backward_local(h)
    for c in range(PARTS):
        arrived(*plans["z2", c])
        state = jnp.zeros((SUB, n), jnp.float32)
        for g in backward:
            y2_send[c, g] = state
            state = z_recv[c, g, SUB : SUB + 1, :] * state + z2_recv[c, g]
        go("y2", c, y2_send, y2_recv, zh)

    for c in range(PARTS):
        arrived(*plans["y2", c])
        later = y2_recv[c].reshape(ROWS, n)
        for i in range(PART_HEADS):
            state = later[part(i)]
            for j in backward:
                b2_send[c, j, part(i), :] = state
                state = decay_of(c, j, i) * state + a2_recv[c, j, part(i), :]
        go("b2", c, b2_send, b2_recv, me)

    for key, p in plans.items():
        if key[0] != "b2":
            sent(*p)

    for c in range(PARTS):
        arrived(*plans["b2", c])
        for i in range(PART_HEADS):
            h = c * PART_HEADS + i
            state = b2_recv[c, :, part(i), :].reshape(n, n).astype(jnp.bfloat16)
            gk_ref[:, cols(h)] = (
                gki_ref[h] + kd_ref[h] * dot(v_ref[:, cols(h)], state, 1, 1)
            ).astype(jnp.bfloat16)
            gv_ref[:, cols(h)] = (gvi_ref[h] + dot(ks_ref[h], state, 1, 0)).astype(jnp.bfloat16)
    for c in range(PARTS):
        sent(*plans["b2", c])


def write_out(*refs):
    sem = refs[8]
    stores = [pltpu.make_async_copy(refs[i], refs[4 + i], sem.at[i]) for i in range(4)]
    for c in stores:
        c.start()
    for c in stores:
        c.wait()


def body(queries, keys, values, log_decay, gain, grad_out):
    n = HEAD_DIM
    shape = queries.shape
    f32, bf16 = jnp.float32, jnp.bfloat16
    hbm = pl.BlockSpec(memory_space=pltpu.HBM)
    vmem = pl.BlockSpec(memory_space=pltpu.VMEM)
    full = pltpu.VMEM(shape, bf16)
    wide = pltpu.VMEM((LOCAL_HEADS, n, n), f32)
    half = pltpu.VMEM((LOCAL_HEADS, n, n), bf16)

    def slots(rows):
        return [pltpu.VMEM((PARTS, 8, rows, n), f32)] * 2

    made = pl.pallas_call(
            kernel,
            out_shape=[jax.ShapeDtypeStruct(shape, bf16)] * 4,
            in_specs=[hbm, hbm, hbm, vmem, vmem, hbm],
            out_specs=[vmem] * 4,
            scratch_shapes=[
                *[full] * 4,
                wide, wide, wide, wide, half, half, half, wide, wide, half, half, wide, wide,
                *slots(ROWS + 8), *slots(SUB + 8), *slots(SUB), *slots(ROWS),
                *slots(ROWS), *slots(SUB), *slots(SUB), *slots(ROWS),
                pltpu.VMEM((8, n), f32), pltpu.VMEM((8, 8, n), f32),
                pltpu.SemaphoreType.DMA((4,)),
                pltpu.SemaphoreType.DMA((8 * PARTS + 1, 7)), pltpu.SemaphoreType.DMA((8 * PARTS + 1, 7)),
                pltpu.SemaphoreType.REGULAR, pltpu.SemaphoreType.REGULAR,
            ],
            compiler_params=pltpu.CompilerParams(
                collective_id=0, has_side_effects=True, vmem_limit_bytes=VMEM_LIMIT
            ),
            cost_estimate=pl.CostEstimate(flops=600_000_000, bytes_accessed=3_000_000, transcendentals=400_000),
        )(queries, keys, values, log_decay.T, gain.reshape(1, -1), grad_out)
    return tuple(
        pl.pallas_call(
            write_out,
            out_shape=[jax.ShapeDtypeStruct(shape, bf16)] * 4,
            in_specs=[pl.BlockSpec(memory_space=pl.ANY)] * 4,
            out_specs=[hbm] * 4,
            scratch_shapes=[pltpu.SemaphoreType.DMA((4,))],
            compiler_params=pltpu.CompilerParams(vmem_limit_bytes=16 * 2**20),
        )(*made)
    )


def solution(mesh):
    finer = Mesh(mesh.devices.reshape(8, 2, 4, mesh.shape["head"]), AXES)
    ctx = ("zh", "zl", "x")
    both = P(ctx, "head")
    return jax.shard_map(
        body,
        mesh=finer,
        in_specs=(both, both, both, both, P("head"), both),
        out_specs=(both,) * 4,
        check_vma=False,
    )
```

```python
import functools

import jax
import jax.numpy as jnp
from jax import lax
from jax.experimental import pallas as pl
from jax.experimental.pallas import tpu as pltpu
from jax.sharding import Mesh
from jax.sharding import PartitionSpec as P

HEADS = 64
HEAD_DIM = 128
GROUP = 8
GROUPS = 8
PARTS = 1
LOCAL_HEADS = 8
PART_HEADS = LOCAL_HEADS // PARTS
SLICE = HEAD_DIM // GROUP
ROWS = PART_HEADS * SLICE
VMEM_LIMIT = 54016 * 1024
SUB = ROWS // GROUPS
FAR_FIRST = (4, 3, 5, 2, 6, 1, 7)
GROUP_FAR_FIRST = (6, 2, 5, 3, 7, 1, 4)
AXES = ("zh", "zl", "x", "head")
MESH = pl.DeviceIdType.MESH

epsilon = 1e-06


def dot(a, b, ca, cb, precision=None):
    return lax.dot_general(
        a, b, (((ca,), (cb,)), ((), ())), preferred_element_type=jnp.float32, precision=precision
    )


def kernel(
    q_hbm, k_hbm, v_hbm, log_ref, gain_ref, g_hbm,
    n_ref, gq_ref, gk_ref, gv_ref,
    q_ref, k_ref, v_ref, g_ref,
    cum_ref, decay_ref, kd_ref, qd_ref, ks_ref, qst_ref, w_ref, att_ref, sg_ref, ga_ref, s_ref, gki_ref, gvi_ref,
    a_send, a_recv, z_send, z_recv, y_send, y_recv, b_send, b_recv,
    a2_send, a2_recv, z2_send, z2_recv, y2_send, y2_recv, b2_send, b2_recv,
    h_send, h_recv, in_sem, send_sem, recv_sem, near_sem, far_sem,
):
    zh, zl, x, head = (lax.axis_index(a) for a in AXES)
    me = zl * 4 + x

    def group_device(j):
        return (zh, lax.div(j, 4), lax.rem(j, 4), head)

    def groups_device(j):
        return (j, zl, x, head)

    def head_device(j):
        return (zh, zl, x, j)

    def copies(src, dst, mine, device, slot, arriving):
        for k in GROUP_FAR_FIRST if device is group_device else FAR_FIRST:
            j = lax.rem(mine + (8 - k if arriving else k), 8)
            yield pltpu.make_async_remote_copy(
                src_ref=src(j),
                dst_ref=dst(j if arriving else mine),
                send_sem=send_sem.at[slot, k - 1],
                recv_sem=recv_sem.at[slot, k - 1],
                device_id=device(j),
                device_id_type=MESH,
            )

    def exchange(src, dst, mine, device, slot):
        for c in copies(src, dst, mine, device, slot, False):
            c.start()

    def arrived(src, dst, mine, device, slot):
        for c in copies(src, dst, mine, device, slot, True):
            c.wait_recv()

    def sent(src, dst, mine, device, slot):
        for c in copies(src, dst, mine, device, slot, False):
            c.wait_send()

    barrier = pltpu.get_barrier_semaphore()
    def tell(sem, mine, device, offsets):
        for k in offsets:
            pl.semaphore_signal(
                sem, inc=1, device_id=device(lax.rem(mine + k, 8)), device_id_type=MESH
            )

    tell(barrier, me, group_device, FAR_FIRST)
    tell(barrier, head, head_device, FAR_FIRST)
    tell(barrier, zh, groups_device, (1, 7))
    loads = [
        pltpu.make_async_copy(a, b, in_sem.at[i])
        for i, (a, b) in enumerate(((k_hbm, k_ref), (v_hbm, v_ref), (q_hbm, q_ref), (g_hbm, g_ref)))
    ]
    for c in loads:
        c.start()

    def cols(h):
        return slice(h * HEAD_DIM, (h + 1) * HEAD_DIM)

    n = HEAD_DIM
    row = lax.broadcasted_iota(jnp.int32, (n, n), 0)
    col = lax.broadcasted_iota(jnp.int32, (n, n), 1)
    upto = jnp.where(row <= col, 1.0, 0.0).astype(jnp.float32)
    cum = dot(log_ref[...], upto, 1, 0, lax.Precision.HIGHEST)
    last = jnp.broadcast_to(cum[:, n - 1 :], (LOCAL_HEADS, n))
    block_decay = jnp.exp(last)

    def across(r):
        return jnp.broadcast_to(r, (n, n))

    def at(ref, c):
        return lambda j: ref.at[c, j]

    plans = {}
    slot = 0
    for name, (s, r, mine, device) in {
        "a": (a_send, a_recv, me, group_device),
        "z": (z_send, z_recv, zh, groups_device),
        "y": (y_send, y_recv, zh, groups_device),
        "b": (b_send, b_recv, me, group_device),
        "a2": (a2_send, a2_recv, me, group_device),
        "z2": (z2_send, z2_recv, zh, groups_device),
        "y2": (y2_send, y2_recv, zh, groups_device),
        "b2": (b2_send, b2_recv, me, group_device),
    }.items():
        for c in range(PARTS):
            plans[name, c] = (at(s, c), at(r, c), mine, device, slot)
            slot += 1
    plans["h"] = (lambda j: h_send, lambda j: h_recv.at[j], head, head_device, slot)

    def go(name, c, s, r, mine):
        r[c, mine] = s[c, mine]
        exchange(*plans[name, c])

    loads[0].wait()
    loads[1].wait()
    for c in range(PARTS):
        for i in range(PART_HEADS):
            h = c * PART_HEADS + i
            cum_col = across(cum[h : h + 1]).T
            key_decay = jnp.exp(last[h : h + 1] - cum_col)
            kd_ref[h] = key_decay
            cum_ref[h] = cum_col
            ks = (key_decay * k_ref[:, cols(h)].astype(jnp.float32)).astype(jnp.bfloat16)
            ks_ref[h] = ks
            state = dot(ks, v_ref[:, cols(h)], 0, 0)
            a_send[c, :, i * SLICE : (i + 1) * SLICE, :] = state.reshape(GROUP, SLICE, n)
        a_send[c, :, ROWS:, :] = jnp.broadcast_to(block_decay[None], (GROUP, LOCAL_HEADS, n))
        if c == 0:
            pl.semaphore_wait(barrier, 16)
            tell(near_sem, zh, groups_device, (1, 7))
        go("a", c, a_send, a_recv, me)

    pl.semaphore_wait(near_sem, 2)
    tell(far_sem, zh, groups_device, (2, 6))
    loads[2].wait()
    loads[3].wait()

    def forward_local(h):
        q = q_ref[:, cols(h)]
        cum_col = cum_ref[h]
        qd_ref[h] = jnp.exp(cum_col)
        decay_ref[h] = jnp.where(
            row >= col, jnp.exp(jnp.minimum(cum_col - across(cum[h : h + 1]), 0.0)), 0.0
        )
        w = (dot(q, k_ref[:, cols(h)], 1, 1) * decay_ref[h]).astype(jnp.bfloat16)
        w_ref[h] = w
        att_ref[h] = dot(w, v_ref[:, cols(h)], 1, 0)

    def forward_more(h):
        qst_ref[h] = (qd_ref[h] * q_ref[:, cols(h)].astype(jnp.float32)).T.astype(jnp.bfloat16)
        sg_ref[h] = g_ref[:, cols(h)].astype(jnp.float32) * gain_ref[:, cols(h)]

    for h in range(LOCAL_HEADS):
        forward_local(h)

    def decay_of(c, j, i):
        h = c * PART_HEADS + i
        return a_recv[c, j, ROWS + h : ROWS + h + 1, :]

    def part(i):
        return slice(i * SLICE, (i + 1) * SLICE)

    forward = range(8)
    backward = range(7, -1, -1)

    pl.semaphore_wait(far_sem, 2)
    for c in range(PARTS):
        arrived(*plans["a", c])
        folded, decays = [], []
        for i in range(PART_HEADS):
            total = a_recv[c, 0, part(i), :]
            decay = decay_of(c, 0, i)
            for j in range(1, GROUP):
                d = decay_of(c, j, i)
                total = d * total + a_recv[c, j, part(i), :]
                decay = d * decay
            folded.append(total)
            decays.append(jnp.broadcast_to(decay, (SLICE * 8 // SUB, n)))
        z_send[c, :, :SUB, :] = jnp.concatenate(folded, axis=0).reshape(GROUPS, SUB, n)
        z_send[c, :, SUB:, :] = jnp.concatenate(decays, axis=0).reshape(GROUPS, 8, n)
        go("z", c, z_send, z_recv, zh)

    for h in range(LOCAL_HEADS):
        forward_more(h)

    for c in range(PARTS):
        arrived(*plans["z", c])
        state = jnp.zeros((SUB, n), jnp.float32)
        for g in forward:
            y_send[c, g] = state
            state = z_recv[c, g, SUB : SUB + 1, :] * state + z_recv[c, g, :SUB, :]
        go("y", c, y_send, y_recv, zh)

    for c in range(PARTS):
        arrived(*plans["y", c])
        entering = y_recv[c].reshape(ROWS, n)
        for i in range(PART_HEADS):
            state = entering[part(i)]
            for j in forward:
                b_send[c, j, part(i), :] = state
                state = decay_of(c, j, i) * state + a_recv[c, j, part(i), :]
        go("b", c, b_send, b_recv, me)

    squares = jnp.zeros((n, n), jnp.float32)
    products = jnp.zeros((n, n), jnp.float32)
    for c in range(PARTS):
        arrived(*plans["b", c])
        for i in range(PART_HEADS):
            h = c * PART_HEADS + i
            state = b_recv[c, :, part(i), :].reshape(n, n).astype(jnp.bfloat16)
            s_ref[h] = state
            att = att_ref[h] + qd_ref[h] * dot(q_ref[:, cols(h)], state, 1, 0)
            att_ref[h] = att
            squares += att * att
            products += sg_ref[h] * att

    sums = jnp.where(
        lax.broadcasted_iota(jnp.int32, (8, n), 0) == 0,
        jnp.sum(squares.T, axis=0, keepdims=True),
        jnp.sum(products.T, axis=0, keepdims=True),
    )
    h_send[...] = sums
    h_recv[head] = sums
    exchange(*plans["h"])
    arrived(*plans["h"])
    sums = h_recv[0]
    for j in range(1, 8):
        sums += h_recv[j]
    width = HEADS * HEAD_DIM
    inverse_row = lax.rsqrt(sums[0:1] / width + epsilon)
    factor_row = inverse_row * inverse_row * inverse_row * sums[1:2] / width
    inverse = across(inverse_row).T
    factor = across(factor_row).T

    for c in range(PARTS):
        for i in range(PART_HEADS):
            h = c * PART_HEADS + i
            ga = (inverse * sg_ref[h] - att_ref[h] * factor).astype(jnp.bfloat16)
            ga_ref[h] = ga
            a2_send[c, :, part(i), :] = dot(qst_ref[h], ga, 1, 0).reshape(GROUP, SLICE, n)
        go("a2", c, a2_send, a2_recv, me)

    def backward_local(h):
        ga = ga_ref[h]
        gs = (dot(ga, v_ref[:, cols(h)], 1, 1) * decay_ref[h]).astype(jnp.bfloat16)
        gq_ref[:, cols(h)] = (
            dot(gs, k_ref[:, cols(h)], 1, 0) + qd_ref[h] * dot(ga, s_ref[h], 1, 1)
        ).astype(jnp.bfloat16)
        gki_ref[h] = dot(gs, q_ref[:, cols(h)], 0, 0)
        gvi_ref[h] = dot(w_ref[h], ga, 0, 0)
        n_ref[:, cols(h)] = (att_ref[h] * inverse * gain_ref[:, cols(h)]).astype(jnp.bfloat16)

    for h in range(PART_HEADS):
        backward_local(h)

    for c in range(PARTS):
        arrived(*plans["a2", c])
        folded = []
        for i in range(PART_HEADS):
            total = a2_recv[c, GROUP - 1, part(i), :]
            for j in range(GROUP - 2, -1, -1):
                total = decay_of(c, j, i) * total + a2_recv[c, j, part(i), :]
            folded.append(total)
        z2_send[c] = jnp.concatenate(folded, axis=0).reshape(GROUPS, SUB, n)
        go("z2", c, z2_send, z2_recv, zh)

    for h in range(PART_HEADS, LOCAL_HEADS):
        backward_local(h)
    for c in range(PARTS):
        arrived(*plans["z2", c])
        state = jnp.zeros((SUB, n), jnp.float32)
        for g in backward:
            y2_send[c, g] = state
            state = z_recv[c, g, SUB : SUB + 1, :] * state + z2_recv[c, g]
        go("y2", c, y2_send, y2_recv, zh)

    for c in range(PARTS):
        arrived(*plans["y2", c])
        later = y2_recv[c].reshape(ROWS, n)
        for i in range(PART_HEADS):
            state = later[part(i)]
            for j in backward:
                b2_send[c, j, part(i), :] = state
                state = decay_of(c, j, i) * state + a2_recv[c, j, part(i), :]
        go("b2", c, b2_send, b2_recv, me)

    for key, p in plans.items():
        if key[0] != "b2":
            sent(*p)

    for c in range(PARTS):
        arrived(*plans["b2", c])
        for i in range(PART_HEADS):
            h = c * PART_HEADS + i
            state = b2_recv[c, :, part(i), :].reshape(n, n).astype(jnp.bfloat16)
            gk_ref[:, cols(h)] = (
                gki_ref[h] + kd_ref[h] * dot(v_ref[:, cols(h)], state, 1, 1)
            ).astype(jnp.bfloat16)
            gv_ref[:, cols(h)] = (gvi_ref[h] + dot(ks_ref[h], state, 1, 0)).astype(jnp.bfloat16)
    for c in range(PARTS):
        sent(*plans["b2", c])


def write_out(*refs):
    sem = refs[8]
    stores = [pltpu.make_async_copy(refs[i], refs[4 + i], sem.at[i]) for i in range(4)]
    for c in stores:
        c.start()
    for c in stores:
        c.wait()


def body(queries, keys, values, log_decay, gain, grad_out):
    n = HEAD_DIM
    shape = queries.shape
    f32, bf16 = jnp.float32, jnp.bfloat16
    hbm = pl.BlockSpec(memory_space=pltpu.HBM)
    vmem = pl.BlockSpec(memory_space=pltpu.VMEM)
    full = pltpu.VMEM(shape, bf16)
    wide = pltpu.VMEM((LOCAL_HEADS, n, n), f32)
    half = pltpu.VMEM((LOCAL_HEADS, n, n), bf16)

    def slots(rows):
        return [pltpu.VMEM((PARTS, 8, rows, n), f32)] * 2

    made = pl.pallas_call(
            kernel,
            out_shape=[jax.ShapeDtypeStruct(shape, bf16)] * 4,
            in_specs=[hbm, hbm, hbm, vmem, vmem, hbm],
            out_specs=[vmem] * 4,
            scratch_shapes=[
                *[full] * 4,
                wide, wide, wide, wide, half, half, half, wide, wide, half, half, wide, wide,
                *slots(ROWS + 8), *slots(SUB + 8), *slots(SUB), *slots(ROWS),
                *slots(ROWS), *slots(SUB), *slots(SUB), *slots(ROWS),
                pltpu.VMEM((8, n), f32), pltpu.VMEM((8, 8, n), f32),
                pltpu.SemaphoreType.DMA((4,)),
                pltpu.SemaphoreType.DMA((8 * PARTS + 1, 7)), pltpu.SemaphoreType.DMA((8 * PARTS + 1, 7)),
                pltpu.SemaphoreType.REGULAR, pltpu.SemaphoreType.REGULAR,
            ],
            compiler_params=pltpu.CompilerParams(
                collective_id=0, has_side_effects=True, vmem_limit_bytes=VMEM_LIMIT
            ),
            cost_estimate=pl.CostEstimate(flops=600_000_000, bytes_accessed=3_000_000, transcendentals=400_000),
        )(queries, keys, values, log_decay.T, gain.reshape(1, -1), grad_out)
    return tuple(
        pl.pallas_call(
            write_out,
            out_shape=[jax.ShapeDtypeStruct(shape, bf16)] * 4,
            in_specs=[pl.BlockSpec(memory_space=pl.ANY)] * 4,
            out_specs=[hbm] * 4,
            scratch_shapes=[pltpu.SemaphoreType.DMA((4,))],
            compiler_params=pltpu.CompilerParams(vmem_limit_bytes=16 * 2**20),
        )(*made)
    )


def solution(mesh):
    finer = Mesh(mesh.devices.reshape(8, 2, 4, mesh.shape["head"]), AXES)
    ctx = ("zh", "zl", "x")
    both = P(ctx, "head")
    return jax.shard_map(
        body,
        mesh=finer,
        in_specs=(both, both, both, both, P("head"), both),
        out_specs=(both,) * 4,
        check_vma=False,
    )
```
